256 devices in a mesh: member: 16 (over x_hi, z), space: 16 (over y, x_lo, core).
Axes of the slice: x: 4 (x_hi: 2, x_lo: 2; x = x_hi * 2 + x_lo), y: 4, z: 8, core: 2. Of those that a mesh axis runs over, the one named last changes fastest.
Arguments:
- alpha: float32 [32, 16, 128, 1280], P('member', None, 'space'), may hold values from -6 to 6
- perturb: bfloat16 [4, 32, 16, 128, 1280], P(None, 'member', None, 'space'), may hold values from -1 to 1
- kappa: float32 [128, 1280], P('space'), may hold values from 0.1 to 0.24
- land: int32 [128, 1280], P('space'), may hold values 0 or 1
- obs_weight: float32 [4, 16, 128, 1280], P(None, 'member', 'space'), may hold values from 0.2 to 5
- innovation: float32 [4, 16, 128, 1280], P(None, 'member', 'space'), may hold values from -6 to 6
Outputs:
- gradient: float32 [32, 16, 128, 1280], P('member', None, 'space')
- weighted_misfit: float32 [4, 16, 128, 1280], P(None, 'member', 'space')
The draws below stay inside these ranges and needn't reach their ends.
All inputs are finite; a program needn't handle non-finite values. No bound on the sum of `land` on one device may be relied on, other than what follows from the above.
Results may differ from the reference program's by a relative error of at most 0.0003.
Values sent between devices are 32-bit elements; how exact they have to be, the bound alone decides.
A program may use at most 64 MiB of HBM per device.

```python
import math
import jax
import jax.numpy as jnp
from jax import lax

FIELDS = 2
LEVELS = 8
SLOTS = 4
STEPS = 4
LON = 1280
MEMBERS = 32
LAT = 128


def set_ends(array, stream_key, low, largest):
    shape = array.shape
    spot = [jax.random.randint(jax.random.fold_in(stream_key, axis), (), 0, shape[axis]) for axis in range(len(shape))]
    array = array.at[tuple(spot)].set(low)
    longest = shape.index(max(shape))
    spot[longest] = (spot[longest] + 1) % shape[longest]
    return array.at[tuple(spot)].set(largest)


def shard_levels(rng, shape, split, least, top_value):
    def one(position, shards_of):
        draws = jax.random.uniform(jax.random.fold_in(jax.random.fold_in(rng, 6), position), (shards_of,), jnp.float32, least / len(split), top_value / len(split))
        return jnp.repeat(jnp.exp(draws), shape[position] // shards_of).reshape((-1,) + (1,) * (len(shape) - position - 1))

    gain = one(*split[0])
    for cut in split[1:]:
        gain = gain * one(*cut)
    return gain


def noise(stream_key, extent, deviation, bound, split=(), kind=jnp.bfloat16):
    level = shard_levels(stream_key, extent, split, -0.22, 0.18) if split else 1.0
    values = jax.random.normal(stream_key, extent, jnp.float32) * deviation * level
    return jnp.minimum(jnp.maximum(values, -bound), bound).astype(kind)


def setup_inputs(seed: int = 0) -> dict:
    arg_keys = jax.random.split(jax.random.key(seed), 7)
    alpha = noise(arg_keys[0], (MEMBERS, FIELDS * LEVELS, LAT, LON), 1.0, 6.0, ((0, 16), (2, 16)), jnp.float32)
    perturb = noise(arg_keys[1], (SLOTS, MEMBERS, FIELDS * LEVELS, LAT, LON), MEMBERS ** -0.5, 1.0, ((1, 16), (3, 16)))
    kappa = jnp.clip(0.1 + 0.13999999 * jax.random.uniform(arg_keys[2], (LAT, LON), jnp.float32) ** shard_levels(arg_keys[2], (LAT, LON), ((0, 16),), -0.2, 0.2), 0.1, 0.24)
    land = set_ends((jax.random.randint(arg_keys[3], (LAT, LON), 0, 4) < 3).astype(jnp.int32), jax.random.fold_in(arg_keys[3], 1), 0, 1)
    obs_weight = jnp.clip(jnp.exp(math.log(5.0) - 3.218876 * jax.random.uniform(arg_keys[4], (SLOTS, FIELDS * LEVELS, LAT, LON), jnp.float32) ** shard_levels(arg_keys[4], (SLOTS, FIELDS * LEVELS, LAT, LON), ((1, 16), (2, 16)), -0.2, 0.2)), 0.2, 5.0)
    innovation = noise(arg_keys[5], (SLOTS, FIELDS * LEVELS, LAT, LON), 1.0, 6.0, ((1, 16), (2, 16)), jnp.float32)
    return {"alpha": alpha, "perturb": perturb, "kappa": kappa, "land": land, "obs_weight": obs_weight, "innovation": innovation}


def face_terms(kappa):
    padded = jnp.pad(kappa, ((1, 1), (0, 0)))
    coef_north = 0.5 * (padded[1:-1] + padded[2:])
    coef_south = 0.5 * (padded[1:-1] + padded[:-2])
    coef_east = 0.5 * (kappa + jnp.roll(kappa, -1, axis=1))
    coef_west = 0.5 * (kappa + jnp.roll(kappa, 1, axis=1))
    return coef_east, coef_west, coef_north, coef_south


def diffuse(field, faces):
    coef_east, coef_west, coef_north, coef_south = faces
    current = field
    for sweep in range(STEPS):
        padded = jnp.pad(current, ((0, 0), (1, 1), (0, 0)))
        current = (current + coef_east * (jnp.roll(current, -1, axis=-1) - current)
                   + coef_west * (jnp.roll(current, 1, axis=-1) - current)
                   + coef_north * (padded[:, 2:, :] - current)
                   + coef_south * (padded[:, :-2, :] - current))
    return current


def reference(alpha, perturb, kappa, land, obs_weight, innovation):
    faces = face_terms(kappa)
    sea = land.astype(jnp.float32)

    def forward(total, member):
        local = diffuse(alpha[member], faces) * sea
        return total + perturb[:, member].astype(jnp.float32) * local[None], None

    start = jnp.zeros(obs_weight.shape, jnp.float32)
    increment, unused = lax.scan(forward, start, jnp.arange(MEMBERS))
    weighted_misfit = obs_weight * (increment - innovation)

    def adjoint(member):
        back = jnp.sum(perturb[:, member].astype(jnp.float32) * weighted_misfit, axis=0)
        return diffuse(back * sea, faces) + alpha[member]

    gradient = lax.map(adjoint, jnp.arange(MEMBERS))
    return gradient, weighted_misfit
```

```python
import jax
import jax.numpy as jnp
from jax import lax
from jax.experimental import pallas as pl
from jax.experimental.pallas import tpu as pltpu
from jax.sharding import PartitionSpec as P

STEPS = 4
ROWS = 8
LON = 1280
HALO = 4
RING = 8
PAIR = 2
SLOTS = 4
OWN = 2
SPACE = 16
MESH = pl.DeviceIdType.MESH
DOWN, UP = 0, 1
REACH = {DOWN: (4, 4, 3, 3), UP: (3, 3, 4, 4)}
NEAR_LAST = (4, -3, 3, -2, 2, -1, 1, 0)


def kernel(
    alpha, perturb, kappa, land, weight, innov,
    grad_out, misfit_out,
    al, pe, halo_f, halo_b, back, result, kap, coef, sea_i, sea,
    local, ring, total, across, obs, misfit,
    in_sem, out_sem, kap_sem, hf_send, hf_recv, hb_send, hb_recv,
    rs_send, rs_recv, x_send, x_recv, ob_send, ob_recv, ag_send, ag_recv,
):
    member = lax.axis_index("member")
    space = lax.axis_index("space")
    pair = member // RING
    depth = lax.rem(member, RING)
    below = (pair * RING + lax.rem(depth + RING - 1, RING), space)
    above = (pair * RING + lax.rem(depth + 1, RING), space)
    opposite = ((1 - pair) * RING + depth, space)
    north = (member, lax.rem(space + 1, SPACE))
    south = (member, lax.rem(space + SPACE - 1, SPACE))
    toward = {DOWN: below, UP: above}

    def at(off):
        return lax.rem(depth + (off + RING), RING)

    def remote(src, dst, send, recv, device):
        return pltpu.make_async_remote_copy(
            src_ref=src, dst_ref=dst, send_sem=send, recv_sem=recv, device_id=device, device_id_type=MESH
        )

    sent = []

    def go(copy):
        copy.start()
        sent.append(copy)

    loads = [
        pltpu.make_async_copy(kappa, kap.at[pl.ds(0, ROWS)], in_sem.at[0]),
        pltpu.make_async_copy(alpha, al, in_sem.at[1]),
        pltpu.make_async_copy(land, sea_i, in_sem.at[2]),
        pltpu.make_async_copy(perturb, pe, in_sem.at[3]),
        pltpu.make_async_copy(weight, obs.at[pair, 0], in_sem.at[4]),
        pltpu.make_async_copy(innov, obs.at[pair, 1], in_sem.at[5]),
    ]
    for load in loads:
        load.start()

    barrier = pltpu.get_barrier_semaphore()
    for device in (below, above, opposite, north, south):
        pl.semaphore_signal(barrier, inc=1, device_id=device, device_id_type=MESH)
    pl.semaphore_wait(barrier, 5)

    low, high = pl.ds(0, HALO), pl.ds(HALO, HALO)
    kap_copies = (
        remote(kappa.at[high], kap.at[pl.ds(ROWS + HALO, HALO)], kap_sem.at[0], kap_sem.at[1], north),
        remote(kappa.at[low], kap.at[pl.ds(ROWS, HALO)], kap_sem.at[2], kap_sem.at[3], south),
    )

    def edges(src, dst, send, recv, off):
        z = at(off)
        j = off % RING
        return (
            remote(src.at[:, :, z, high], dst.at[:, :, z, high], send.at[j, 0], recv.at[j, 0], north),
            remote(src.at[:, :, z, low], dst.at[:, :, z, low], send.at[j, 1], recv.at[j, 1], south),
        )

    forward = {off: edges(alpha, halo_f, hf_send, hf_recv, off) for off in NEAR_LAST}
    backward = {off: edges(back, halo_b, hb_send, hb_recv, off) for off in NEAR_LAST}
    observed = (
        remote(weight, obs.at[pair, 0], ob_send.at[0], ob_recv.at[0], opposite),
        remote(innov, obs.at[pair, 1], ob_send.at[1], ob_recv.at[1], opposite),
    )
    scatter = {
        (way, k, t): remote(
            ring.at[way, k, t], ring.at[way, k - 1, t],
            rs_send.at[way, k - 1, t], rs_recv.at[way, k - 1, t], toward[way],
        )
        for way in (DOWN, UP) for t in range(SLOTS) for k in range(1, REACH[way][t] + 1)
    }
    cross = [remote(total.at[t], across.at[t], x_send.at[t], x_recv.at[t], opposite) for t in range(SLOTS)]

    def gather_copy(way, k, t):
        z = at(k if way == DOWN else -k)
        return remote(
            misfit.at[z, t], misfit.at[z, t], ag_send.at[way, k, t], ag_recv.at[way, k, t], toward[way]
        )

    gather = {
        (way, k, t): gather_copy(way, k, t)
        for way in (DOWN, UP) for t in range(SLOTS) for k in range(REACH[way][t])
    }

    def send_edges(copies):
        for copy in copies:
            go(copy)

    send_edges(kap_copies)
    send_edges(forward[NEAR_LAST[0]])
    send_edges(forward[NEAR_LAST[1]])

    loads[0].wait()
    for copy in kap_copies:
        copy.wait_recv()
    row = lax.broadcasted_iota(jnp.int32, (2 * ROWS, LON), 0)
    inside = (row < ROWS) | ((row < ROWS + HALO) & (space < SPACE - 1)) | ((row >= ROWS + HALO) & (space > 0))
    k16 = jnp.where(inside, kap[...], 0.0)
    east = 0.5 * (k16 + pltpu.roll(k16, LON - 1, 1))
    west = 0.5 * (k16 + pltpu.roll(k16, 1, 1))
    up = 0.5 * (k16 + pltpu.roll(k16, 2 * ROWS - 1, 0))
    down = 0.5 * (k16 + pltpu.roll(k16, 1, 0))
    for i, c in enumerate((1.0 - (east + west + up + down), east, west, up, down)):
        coef[i] = jnp.where(inside, c, 0.0)
    loads[2].wait()
    sea[...] = sea_i[...].astype(jnp.float32)

    def smooth(tile, edge):
        row8 = lax.broadcasted_iota(jnp.int32, (ROWS, LON), 0)
        known = ((row8 < HALO) & (space < SPACE - 1)) | ((row8 >= HALO) & (space > 0))
        u = jnp.concatenate([tile, jnp.where(known, edge, 0.0)], axis=0)
        for step in range(STEPS):
            n = 2 * ROWS if step < STEPS - 1 else ROWS
            terms = (
                u,
                pltpu.roll(u, LON - 1, 1),
                pltpu.roll(u, 1, 1),
                pltpu.roll(u, 2 * ROWS - 1, 0),
                pltpu.roll(u, 1, 0),
            )
            acc = coef[0, :n] * terms[0][:n]
            for i in range(1, 5):
                acc = acc + coef[i, :n] * terms[i][:n]
            u = acc
        return u

    def diffuse_forward(off):
        for copy in forward[off]:
            copy.wait_recv()
        z = at(off)

        @pl.loop(0, OWN * PAIR)
        def _(i):
            m, p = i // PAIR, lax.rem(i, PAIR)
            local[m, p, z] = smooth(al[m, p, z], halo_f[m, p, z]) * sea[...]

    def partial(off, t, p):
        z = at(off)
        return (
            pe[t, 0, p, z].astype(jnp.float32) * local[0, p, z]
            + pe[t, 1, p, z].astype(jnp.float32) * local[1, p, z]
        )

    def scatter_step(way, k, t):
        off = -k if way == DOWN else k
        if k < REACH[way][t]:
            scatter[way, k + 1, t].wait_recv()
        for p in range(PAIR):
            part = partial(off, t, p)
            if k < REACH[way][t]:
                part = part + ring[way, k, t, p]
            ring[way, k, t, p] = part
        go(scatter[way, k, t])

    def cross_step(t):
        for way in (DOWN, UP):
            scatter[way, 1, t].wait_recv()
        for p in range(PAIR):
            total[t, p] = partial(0, t, p) + ring[DOWN, 0, t, p] + ring[UP, 0, t, p]
        go(cross[t])

    stored = []

    def misfit_step(t):
        cross[t].wait_recv()
        for p in range(PAIR):
            misfit[depth, t, p] = obs[p, 0, t] * (total[t, p] + across[t, p] - obs[p, 1, t])
        for way in (DOWN, UP):
            go(gather[way, 0, t])
        copy = pltpu.make_async_copy(misfit.at[depth, t, pair], misfit_out.at[t], out_sem.at[RING + t])
        copy.start()
        stored.append(copy)

    def relay(way, k, t):
        gather[way, k - 1, t].wait_recv()
        if k < REACH[way][t]:
            go(gather[way, k, t])

    def adjoint(off):
        z = at(off)

        @pl.loop(0, OWN * PAIR)
        def _(i):
            m, p = i // PAIR, lax.rem(i, PAIR)
            acc = pe[0, m, p, z].astype(jnp.float32) * misfit[z, 0, p]
            for t in range(1, SLOTS):
                acc = acc + pe[t, m, p, z].astype(jnp.float32) * misfit[z, t, p]
            back[m, p, z] = acc * sea[...]

        send_edges(backward[off])

    def diffuse_backward(off):
        for copy in backward[off]:
            copy.wait_recv()
        z = at(off)

        @pl.loop(0, OWN * PAIR)
        def _(i):
            m, p = i // PAIR, lax.rem(i, PAIR)
            result[m, p, z] = smooth(back[m, p, z], halo_b[m, p, z]) + al[m, p, z]

        copy = pltpu.make_async_copy(result.at[:, :, z], grad_out.at[:, :, z], out_sem.at[off % RING])
        copy.start()
        stored.append(copy)

    a, b, c, d = range(SLOTS)
    loads[1].wait()
    diffuse_forward(4)
    send_edges(forward[3])
    loads[3].wait()
    for way, t in ((DOWN, a), (UP, c), (DOWN, b), (UP, d)):
        scatter_step(way, 4, t)
    diffuse_forward(-3)
    send_edges(forward[-2])
    for t in (c, d):
        scatter_step(DOWN, 3, t)
    diffuse_forward(3)
    send_edges(forward[2])
    for t in (a, b):
        scatter_step(UP, 3, t)
    for t1, t2 in ((a, c), (b, d)):
        scatter_step(DOWN, 3, t1)
        scatter_step(UP, 3, t2)
    diffuse_forward(-2)
    send_edges(forward[-1])
    for t in (c, d):
        scatter_step(DOWN, 2, t)
    diffuse_forward(2)
    send_edges(forward[1])
    for t in (c, d):
        scatter_step(UP, 2, t)
    for t in (a, b):
        scatter_step(DOWN, 2, t)
        scatter_step(UP, 2, t)
    diffuse_forward(-1)
    send_edges(forward[0])
    diffuse_forward(1)
    for t in (c, d, a, b):
        scatter_step(DOWN, 1, t)
        scatter_step(UP, 1, t)
    send_edges(observed)
    diffuse_forward(0)
    loads[4].wait()
    loads[5].wait()
    cross_step(c)
    cross_step(d)
    for copy in observed:
        copy.wait_recv()
    misfit_step(c)
    misfit_step(d)
    cross_step(a)
    cross_step(b)
    misfit_step(a)
    misfit_step(b)
    for k in range(1, 5):
        for t in (c, d, a, b):
            for way in (DOWN, UP):
                if k <= REACH[way][t]:
                    relay(way, k, t)
        if k == 1:
            adjoint(0)
            for off in (1, -1):
                adjoint(off)
            diffuse_backward(0)
        elif k < 4:
            for off in (k, -k):
                adjoint(off)
            for off in (k - 1, 1 - k):
                diffuse_backward(off)
        else:
            adjoint(4)
            for off in (3, -3, 4):
                diffuse_backward(off)

    for copy in sent:
        copy.wait_send()
    for copy in stored:
        copy.wait()


def body(alpha, perturb, kappa, land, obs_weight, innovation):
    f32, dma = jnp.float32, pltpu.SemaphoreType.DMA
    field = (OWN, PAIR, RING, ROWS, LON)
    slab = (SLOTS, PAIR, ROWS, LON)
    anywhere = pl.BlockSpec(memory_space=pl.ANY)
    grad, misfit = pl.pallas_call(
        kernel,
        out_shape=(
            jax.ShapeDtypeStruct(field, f32),
            jax.ShapeDtypeStruct((SLOTS, ROWS, LON), f32),
        ),
        in_specs=[anywhere] * 6,
        out_specs=(anywhere, anywhere),
        scratch_shapes=[
            pltpu.VMEM(field, f32),
            pltpu.VMEM((SLOTS,) + field, jnp.bfloat16),
            pltpu.VMEM(field, f32),
            pltpu.VMEM(field, f32),
            pltpu.VMEM(field, f32),
            pltpu.VMEM(field, f32),
            pltpu.VMEM((2 * ROWS, LON), f32),
            pltpu.VMEM((5, 2 * ROWS, LON), f32),
            pltpu.VMEM((ROWS, LON), jnp.int32),
            pltpu.VMEM((ROWS, LON), f32),
            pltpu.VMEM(field, f32),
            pltpu.VMEM((2, 5) + slab, f32),
            pltpu.VMEM(slab, f32),
            pltpu.VMEM(slab, f32),
            pltpu.VMEM((PAIR, 2, SLOTS, ROWS, LON), f32),
            pltpu.VMEM((RING,) + slab, f32),
            dma((6,)),
            dma((RING + SLOTS,)),
            dma((4,)),
            dma((RING, 2)),
            dma((RING, 2)),
            dma((RING, 2)),
            dma((RING, 2)),
            dma((2, 4, SLOTS)),
            dma((2, 4, SLOTS)),
            dma((SLOTS,)),
            dma((SLOTS,)),
            dma((2,)),
            dma((2,)),
            dma((2, 4, SLOTS)),
            dma((2, 4, SLOTS)),
        ],
        compiler_params=pltpu.CompilerParams(
            collective_id=0, has_side_effects=True, vmem_limit_bytes=40 * 2**20
        ),
    )(
        alpha.reshape(field),
        perturb.reshape((SLOTS,) + field),
        kappa,
        land,
        obs_weight.reshape(SLOTS, ROWS, LON),
        innovation.reshape(SLOTS, ROWS, LON),
    )
    return grad.reshape(alpha.shape), misfit.reshape(obs_weight.shape)


def solution(mesh):
    placed = (
        P("member", None, "space", None),
        P(None, "member", None, "space", None),
        P("space", None),
        P("space", None),
        P(None, "member", "space", None),
        P(None, "member", "space", None),
    )
    return jax.shard_map(
        body,
        mesh=mesh,
        in_specs=placed,
        out_specs=(P("member", None, "space", None), P(None, "member", "space", None)),
        check_vma=False,
    )
```

```python
import jax
import jax.numpy as jnp
from jax import lax
from jax.experimental import pallas as pl
from jax.experimental.pallas import tpu as pltpu
from jax.sharding import PartitionSpec as P

STEPS = 4
ROWS = 8
LON = 1280
HALO = 4
RING = 8
PAIR = 2
SLOTS = 4
OWN = 2
SPACE = 16
FIELDS = tuple((m, p) for m in range(OWN) for p in range(PAIR))
MESH = pl.DeviceIdType.MESH
DOWN, UP = 0, 1
REACH = {DOWN: (4, 4, 3, 3), UP: (3, 3, 4, 4)}
NEAR_LAST = (4, -3, 3, -2, 2, -1, 1, 0)

ORDER = (
    ("load", 1), ("forward", 4), ("edges", -2), ("load", 3), ("scatter", 0, 4, 0), ("scatter", 1, 4, 2),
    ("scatter", 0, 4, 1), ("scatter", 1, 4, 3), ("forward", -3), ("edges", 2), ("scatter", 0, 3, 2),
    ("scatter", 0, 3, 3), ("forward", 3), ("edges", -1), ("scatter", 1, 3, 0), ("forward", -2), ("edges", 1),
    ("scatter", 1, 3, 2), ("scatter", 0, 3, 0), ("forward", 2), ("edges", 0), ("scatter", 1, 3, 3),
    ("scatter", 1, 3, 1), ("observe",), ("forward", -1), ("scatter", 0, 2, 2), ("forward", 1), ("scatter", 0, 2, 3),
    ("scatter", 1, 2, 2), ("scatter", 0, 3, 1), ("forward", 0), ("scatter", 1, 2, 3), ("scatter", 0, 2, 0),
    ("scatter", 1, 2, 0), ("scatter", 0, 1, 2), ("scatter", 0, 1, 3), ("scatter", 1, 1, 2), ("scatter", 0, 2, 1),
    ("scatter", 1, 1, 3), ("scatter", 1, 2, 1), ("scatter", 0, 1, 0), ("scatter", 1, 1, 0), ("observed",),
    ("cross", 2), ("cross", 3), ("scatter", 0, 1, 1), ("scatter", 1, 1, 1), ("load", 5), ("load", 4), ("misfit", 2),
    ("cross", 0), ("misfit", 3), ("cross", 1), ("relay", 0, 1, 2), ("relay", 1, 1, 2), ("misfit", 0),
    ("relay", 0, 1, 3), ("relay", 1, 1, 3), ("misfit", 1), ("adjoint", 0), ("relay", 0, 2, 2), ("relay", 1, 2, 2),
    ("relay", 0, 1, 0), ("relay", 1, 1, 0), ("backward", 0), ("relay", 0, 2, 3), ("relay", 1, 2, 3),
    ("relay", 0, 1, 1), ("adjoint", 1), ("relay", 1, 1, 1), ("adjoint", -1), ("relay", 0, 3, 2), ("relay", 1, 3, 2),
    ("relay", 0, 2, 0), ("relay", 1, 2, 0), ("backward", 1), ("relay", 0, 3, 3), ("relay", 1, 3, 3), ("backward", -1),
    ("relay", 0, 2, 1), ("relay", 1, 2, 1), ("adjoint", -2), ("adjoint", 2), ("relay", 0, 3, 0), ("relay", 1, 4, 2),
    ("relay", 1, 3, 0), ("relay", 0, 3, 1), ("adjoint", 3), ("backward", -2), ("relay", 0, 4, 0), ("relay", 1, 4, 3),
    ("backward", 2), ("relay", 1, 3, 1), ("adjoint", -3), ("relay", 0, 4, 1), ("adjoint", 4), ("backward", 3),
    ("backward", -3), ("backward", 4),
)


def kernel(
    alpha, perturb, kappa, land, weight, innov,
    grad_out, misfit_out,
    al, pe, halo_f, halo_b, back, result, kap, coef, sea_i, sea,
    local, ring, total, across, obs, misfit,
    in_sem, out_sem, kap_sem, hf_send, hf_recv, hb_send, hb_recv,
    rs_send, rs_recv, x_send, x_recv, ob_send, ob_recv, ag_send, ag_recv,
):
    member = lax.axis_index("member")
    space = lax.axis_index("space")
    pair = member // RING
    depth = lax.rem(member, RING)
    below = (pair * RING + lax.rem(depth + RING - 1, RING), space)
    above = (pair * RING + lax.rem(depth + 1, RING), space)
    opposite = ((1 - pair) * RING + depth, space)
    north = (member, lax.rem(space + 1, SPACE))
    south = (member, lax.rem(space + SPACE - 1, SPACE))
    toward = {DOWN: below, UP: above}

    def at(off):
        return lax.rem(depth + (off + RING), RING)

    def remote(src, dst, send, recv, device):
        return pltpu.make_async_remote_copy(
            src_ref=src, dst_ref=dst, send_sem=send, recv_sem=recv, device_id=device, device_id_type=MESH
        )

    sent = []

    def go(copy):
        copy.start()
        sent.append(copy)

    barrier = pltpu.get_barrier_semaphore()
    for device in (below, above, opposite, north, south):
        pl.semaphore_signal(barrier, inc=1, device_id=device, device_id_type=MESH)
    loads = [
        pltpu.make_async_copy(kappa, kap.at[pl.ds(0, ROWS)], in_sem.at[0]),
        pltpu.make_async_copy(alpha, al, in_sem.at[1]),
        pltpu.make_async_copy(land, sea_i, in_sem.at[2]),
        pltpu.make_async_copy(perturb, pe, in_sem.at[3]),
        pltpu.make_async_copy(weight, obs.at[pair, 0], in_sem.at[4]),
        pltpu.make_async_copy(innov, obs.at[pair, 1], in_sem.at[5]),
    ]
    for load in loads:
        load.start()

    pl.semaphore_wait(barrier, 5)

    low, high = pl.ds(0, HALO), pl.ds(HALO, HALO)
    kap_copies = (
        remote(kappa.at[high], kap.at[pl.ds(ROWS + HALO, HALO)], kap_sem.at[0], kap_sem.at[1], north),
        remote(kappa.at[low], kap.at[pl.ds(ROWS, HALO)], kap_sem.at[2], kap_sem.at[3], south),
    )

    def edges(src, dst, send, recv, off):
        z = at(off)
        j = off % RING
        return (
            remote(src.at[:, :, z, high], dst.at[:, :, z, high], send.at[j, 0], recv.at[j, 0], north),
            remote(src.at[:, :, z, low], dst.at[:, :, z, low], send.at[j, 1], recv.at[j, 1], south),
        )

    forward = {off: edges(alpha, halo_f, hf_send, hf_recv, off) for off in NEAR_LAST}
    backward = {off: edges(back, halo_b, hb_send, hb_recv, off) for off in NEAR_LAST}
    observed = (
        remote(weight, obs.at[pair, 0], ob_send.at[0], ob_recv.at[0], opposite),
        remote(innov, obs.at[pair, 1], ob_send.at[1], ob_recv.at[1], opposite),
    )
    scatter = {
        (way, k, t): remote(
            ring.at[way, k, t], ring.at[way, k - 1, t],
            rs_send.at[way, k - 1, t], rs_recv.at[way, k - 1, t], toward[way],
        )
        for way in (DOWN, UP) for t in range(SLOTS) for k in range(1, REACH[way][t] + 1)
    }
    cross = [remote(total.at[t], across.at[t], x_send.at[t], x_recv.at[t], opposite) for t in range(SLOTS)]

    def gather_copy(way, k, t):
        z = at(k if way == DOWN else -k)
        return remote(
            misfit.at[z, t], misfit.at[z, t], ag_send.at[way, k, t], ag_recv.at[way, k, t], toward[way]
        )

    gather = {
        (way, k, t): gather_copy(way, k, t)
        for way in (DOWN, UP) for t in range(SLOTS) for k in range(REACH[way][t])
    }

    def send_edges(copies):
        for copy in copies:
            go(copy)

    send_edges(kap_copies)
    send_edges(forward[NEAR_LAST[0]])

    loads[0].wait()
    for copy in kap_copies:
        copy.wait_recv()
    send_edges(forward[NEAR_LAST[1]])
    row = lax.broadcasted_iota(jnp.int32, (2 * ROWS, LON), 0)
    inside = (row < ROWS) | ((row < ROWS + HALO) & (space < SPACE - 1)) | ((row >= ROWS + HALO) & (space > 0))
    k16 = jnp.where(inside, kap[...], 0.0)
    east = 0.5 * (k16 + pltpu.roll(k16, LON - 1, 1))
    west = 0.5 * (k16 + pltpu.roll(k16, 1, 1))
    up = 0.5 * (k16 + pltpu.roll(k16, 2 * ROWS - 1, 0))
    down = 0.5 * (k16 + pltpu.roll(k16, 1, 0))
    for i, c in enumerate((1.0 - (east + west + up + down), east, west, up, down)):
        coef[i] = jnp.where(inside, c, 0.0)
    send_edges(forward[NEAR_LAST[2]])
    loads[2].wait()
    sea[...] = sea_i[...].astype(jnp.float32)

    def smooth(tile, edge):
        row8 = lax.broadcasted_iota(jnp.int32, (ROWS, LON), 0)
        known = ((row8 < HALO) & (space < SPACE - 1)) | ((row8 >= HALO) & (space > 0))
        u = jnp.concatenate([tile, jnp.where(known, edge, 0.0)], axis=0)
        for step in range(STEPS):
            n = 2 * ROWS if step < STEPS - 1 else ROWS
            terms = (
                u,
                pltpu.roll(u, LON - 1, 1),
                pltpu.roll(u, 1, 1),
                pltpu.roll(u, 2 * ROWS - 1, 0),
                pltpu.roll(u, 1, 0),
            )
            acc = coef[0, :n] * terms[0][:n]
            for i in range(1, 5):
                acc = acc + coef[i, :n] * terms[i][:n]
            u = acc
        return u

    def diffuse_forward(off):
        for copy in forward[off]:
            copy.wait_recv()
        z = at(off)

        @pl.loop(0, OWN * PAIR)
        def _(i):
            m, p = i // PAIR, lax.rem(i, PAIR)
            local[m, p, z] = smooth(al[m, p, z], halo_f[m, p, z]) * sea[...]

    def partial(off, t, p):
        z = at(off)
        return (
            pe[t, 0, p, z].astype(jnp.float32) * local[0, p, z]
            + pe[t, 1, p, z].astype(jnp.float32) * local[1, p, z]
        )

    def scatter_step(way, k, t):
        off = -k if way == DOWN else k
        if k < REACH[way][t]:
            scatter[way, k + 1, t].wait_recv()
        for p in range(PAIR):
            part = partial(off, t, p)
            if k < REACH[way][t]:
                part = part + ring[way, k, t, p]
            ring[way, k, t, p] = part
        go(scatter[way, k, t])

    def cross_step(t):
        for way in (DOWN, UP):
            scatter[way, 1, t].wait_recv()
        for p in range(PAIR):
            total[t, p] = partial(0, t, p) + ring[DOWN, 0, t, p] + ring[UP, 0, t, p]
        go(cross[t])

    stored = []

    def misfit_step(t):
        cross[t].wait_recv()
        for p in range(PAIR):
            misfit[depth, t, p] = obs[p, 0, t] * (total[t, p] + across[t, p] - obs[p, 1, t])
        for way in (DOWN, UP):
            go(gather[way, 0, t])
        copy = pltpu.make_async_copy(misfit.at[depth, t, pair], misfit_out.at[t], out_sem.at[RING + t])
        copy.start()
        stored.append(copy)

    def relay(way, k, t):
        gather[way, k - 1, t].wait_recv()
        if k < REACH[way][t]:
            go(gather[way, k, t])

    def adjoint(off):
        z = at(off)

        @pl.loop(0, OWN * PAIR)
        def _(i):
            m, p = i // PAIR, lax.rem(i, PAIR)
            acc = pe[0, m, p, z].astype(jnp.float32) * misfit[z, 0, p]
            for t in range(1, SLOTS):
                acc = acc + pe[t, m, p, z].astype(jnp.float32) * misfit[z, t, p]
            back[m, p, z] = acc * sea[...]

        send_edges(backward[off])

    def diffuse_backward(off):
        for copy in backward[off]:
            copy.wait_recv()
        z = at(off)

        @pl.loop(0, OWN * PAIR)
        def _(i):
            m, p = i // PAIR, lax.rem(i, PAIR)
            result[m, p, z] = smooth(back[m, p, z], halo_b[m, p, z]) + al[m, p, z]

        copy = pltpu.make_async_copy(result.at[:, :, z], grad_out.at[:, :, z], out_sem.at[off % RING])
        copy.start()
        stored.append(copy)

    tasks = {
        "load": lambda i: loads[i].wait(),
        "edges": lambda off: send_edges(forward[off]),
        "forward": diffuse_forward,
        "scatter": scatter_step,
        "observe": lambda: send_edges(observed),
        "observed": lambda: [copy.wait_recv() for copy in observed],
        "cross": cross_step,
        "misfit": misfit_step,
        "relay": relay,
        "adjoint": adjoint,
        "backward": diffuse_backward,
    }
    for name, *details in ORDER:
        tasks[name](*details)

    for copy in sent:
        copy.wait_send()
    for copy in stored:
        copy.wait()


def finish(grad, misfit, grad_out, misfit_out, held, held_misfit, in_sem, out_sem):
    routes = [(misfit, held_misfit, misfit_out)]
    routes += [(grad.at[m, p], held.at[m, p], grad_out.at[m, p]) for m, p in FIELDS]
    arrive = [pltpu.make_async_copy(a, b, in_sem.at[i]) for i, (a, b, c) in enumerate(routes)]
    leave = [pltpu.make_async_copy(b, c, out_sem.at[i]) for i, (a, b, c) in enumerate(routes)]
    for copy in arrive:
        copy.start()
    for first, second in zip(arrive, leave):
        first.wait()
        second.start()
    for copy in leave:
        copy.wait()


def body(alpha, perturb, kappa, land, obs_weight, innovation):
    f32, dma = jnp.float32, pltpu.SemaphoreType.DMA
    field = (OWN, PAIR, RING, ROWS, LON)
    slab = (SLOTS, PAIR, ROWS, LON)
    anywhere = pl.BlockSpec(memory_space=pltpu.HBM)
    grad, misfit = pl.pallas_call(
        kernel,
        out_shape=(
            jax.ShapeDtypeStruct(field, f32),
            jax.ShapeDtypeStruct((SLOTS, ROWS, LON), f32),
        ),
        in_specs=[anywhere] * 6,
        out_specs=(anywhere, anywhere),
        scratch_shapes=[
            pltpu.VMEM(field, f32),
            pltpu.VMEM((SLOTS,) + field, jnp.bfloat16),
            pltpu.VMEM(field, f32),
            pltpu.VMEM(field, f32),
            pltpu.VMEM(field, f32),
            pltpu.VMEM(field, f32),
            pltpu.VMEM((2 * ROWS, LON), f32),
            pltpu.VMEM((5, 2 * ROWS, LON), f32),
            pltpu.VMEM((ROWS, LON), jnp.int32),
            pltpu.VMEM((ROWS, LON), f32),
            pltpu.VMEM(field, f32),
            pltpu.VMEM((2, 5) + slab, f32),
            pltpu.VMEM(slab, f32),
            pltpu.VMEM(slab, f32),
            pltpu.VMEM((PAIR, 2, SLOTS, ROWS, LON), f32),
            pltpu.VMEM((RING,) + slab, f32),
            dma((6,)),
            dma((RING + SLOTS,)),
            dma((4,)),
            dma((RING, 2)),
            dma((RING, 2)),
            dma((RING, 2)),
            dma((RING, 2)),
            dma((2, 4, SLOTS)),
            dma((2, 4, SLOTS)),
            dma((SLOTS,)),
            dma((SLOTS,)),
            dma((2,)),
            dma((2,)),
            dma((2, 4, SLOTS)),
            dma((2, 4, SLOTS)),
        ],
        compiler_params=pltpu.CompilerParams(
            collective_id=0, has_side_effects=True, vmem_limit_bytes=60 * 2**20
        ),
    )(
        alpha.reshape(field),
        perturb.reshape((SLOTS,) + field),
        kappa,
        land,
        obs_weight.reshape(SLOTS, ROWS, LON),
        innovation.reshape(SLOTS, ROWS, LON),
    )
    grad, misfit = pl.pallas_call(
        finish,
        out_shape=(
            jax.ShapeDtypeStruct(field, f32),
            jax.ShapeDtypeStruct((SLOTS, ROWS, LON), f32),
        ),
        in_specs=[anywhere] * 2,
        out_specs=(anywhere, anywhere),
        scratch_shapes=[
            pltpu.VMEM(field, f32),
            pltpu.VMEM((SLOTS, ROWS, LON), f32),
            dma((len(FIELDS) + 1,)),
            dma((len(FIELDS) + 1,)),
        ],
        compiler_params=pltpu.CompilerParams(vmem_limit_bytes=60 * 2**20),
    )(grad, misfit)
    return grad.reshape(alpha.shape), misfit.reshape(obs_weight.shape)


def solution(mesh):
    placed = (
        P("member", None, "space", None),
        P(None, "member", None, "space", None),
        P("space", None),
        P("space", None),
        P(None, "member", "space", None),
        P(None, "member", "space", None),
    )
    return jax.shard_map(
        body,
        mesh=mesh,
        in_specs=placed,
        out_specs=(P("member", None, "space", None), P(None, "member", "space", None)),
        check_vma=False,
    )
```

```python
import jax
import jax.numpy as jnp
from jax import lax
from jax.experimental import pallas as pl
from jax.experimental.pallas import tpu as pltpu
from jax.sharding import PartitionSpec as P

STEPS = 4
ROWS = 8
LON = 1280
HALO = 4
RING = 8
PAIR = 2
SLOTS = 4
OWN = 2
SPACE = 16
LANES = 128
FIRST = 4
FIELDS = tuple((m, p) for m in range(OWN) for p in range(PAIR))
MESH = pl.DeviceIdType.MESH
DOWN, UP = 0, 1
REACH = {DOWN: (4, 4, 3, 3), UP: (3, 3, 4, 4)}
NEAR_LAST = (4, -3, 3, -2, 2, -1, 1, 0)

ORDER = (
    ("load", 1), ("forward", 4), ("edges", -2), ("load", 3), ("scatter", 0, 4, 0), ("scatter", 1, 4, 2),
    ("scatter", 0, 4, 1), ("scatter", 1, 4, 3), ("forward", -3), ("edges", 2), ("scatter", 0, 3, 2),
    ("scatter", 0, 3, 3), ("forward", 3), ("edges", -1), ("scatter", 1, 3, 0), ("scatter", 0, 3, 0),
    ("scatter", 1, 3, 2), ("forward", -2), ("edges", 1), ("scatter", 1, 3, 3), ("scatter", 1, 3, 1), ("forward", 2),
    ("edges", 0), ("observe",), ("scatter", 0, 2, 2), ("forward", -1), ("scatter", 0, 2, 3), ("scatter", 1, 2, 2),
    ("scatter", 0, 3, 1), ("forward", 1), ("scatter", 0, 2, 0), ("scatter", 1, 2, 3), ("scatter", 1, 2, 0),
    ("forward", 0), ("scatter", 0, 1, 2), ("scatter", 0, 1, 3), ("scatter", 1, 1, 2), ("scatter", 0, 2, 1),
    ("scatter", 1, 1, 3), ("scatter", 1, 2, 1), ("scatter", 0, 1, 0), ("scatter", 1, 1, 0), ("observed",),
    ("cross", 2), ("cross", 3), ("scatter", 0, 1, 1), ("scatter", 1, 1, 1), ("load", 5), ("load", 4), ("misfit", 2),
    ("cross", 0), ("misfit", 3), ("cross", 1), ("relay", 0, 1, 2), ("relay", 1, 1, 2), ("misfit", 0),
    ("relay", 0, 1, 3), ("relay", 1, 1, 3), ("misfit", 1), ("adjoint", 0), ("relay", 0, 2, 2), ("relay", 1, 2, 2),
    ("relay", 0, 1, 0), ("relay", 1, 1, 0), ("backward", 0), ("relay", 0, 2, 3), ("relay", 1, 2, 3),
    ("relay", 0, 1, 1), ("adjoint", 1), ("relay", 1, 1, 1), ("adjoint", -1), ("relay", 0, 3, 2), ("relay", 1, 3, 2),
    ("relay", 0, 2, 0), ("relay", 1, 2, 0), ("backward", 1), ("relay", 0, 3, 3), ("relay", 1, 3, 3), ("backward", -1),
    ("relay", 0, 2, 1), ("adjoint", 2), ("relay", 1, 2, 1), ("adjoint", -2), ("relay", 0, 3, 0), ("relay", 1, 4, 2),
    ("relay", 1, 3, 0), ("relay", 0, 3, 1), ("adjoint", 3), ("backward", 2), ("relay", 1, 4, 3), ("relay", 0, 4, 0),
    ("backward", -2), ("relay", 1, 3, 1), ("adjoint", -3), ("relay", 0, 4, 1), ("adjoint", 4), ("backward", 3),
    ("backward", -3), ("backward", 4),
)


def kernel(
    alpha, perturb, kappa, land, weight, innov,
    grad_out, misfit_out,
    al, pe, halo_f, halo_b, back, result, work, kap, coef, coef_own, sea_i, sea,
    local, ring, total, across, obs, misfit,
    in_sem, out_sem, kap_sem, hf_send, hf_recv, hb_send, hb_recv,
    rs_send, rs_recv, x_send, x_recv, ob_send, ob_recv, ag_send, ag_recv,
):
    member = lax.axis_index("member")
    space = lax.axis_index("space")
    pair = member // RING
    depth = lax.rem(member, RING)
    below = (pair * RING + lax.rem(depth + RING - 1, RING), space)
    above = (pair * RING + lax.rem(depth + 1, RING), space)
    opposite = ((1 - pair) * RING + depth, space)
    north = (member, lax.rem(space + 1, SPACE))
    south = (member, lax.rem(space + SPACE - 1, SPACE))
    toward = {DOWN: below, UP: above}

    def at(off):
        return lax.rem(depth + (off + RING), RING)

    def remote(src, dst, send, recv, device):
        return pltpu.make_async_remote_copy(
            src_ref=src, dst_ref=dst, send_sem=send, recv_sem=recv, device_id=device, device_id_type=MESH
        )

    sent = []

    def go(copy):
        copy.start()
        sent.append(copy)

    barrier = pltpu.get_barrier_semaphore()
    for device in (below, above, opposite, north, south):
        pl.semaphore_signal(barrier, inc=1, device_id=device, device_id_type=MESH)
    loads = [
        pltpu.make_async_copy(kappa, kap.at[pl.ds(HALO, ROWS)], in_sem.at[0]),
        pltpu.make_async_copy(alpha, al, in_sem.at[1]),
        pltpu.make_async_copy(land, sea_i, in_sem.at[2]),
        pltpu.make_async_copy(perturb, pe, in_sem.at[3]),
        pltpu.make_async_copy(weight, obs.at[pair, 0], in_sem.at[4]),
        pltpu.make_async_copy(innov, obs.at[pair, 1], in_sem.at[5]),
    ]
    for load in loads:
        load.start()

    work[...] = jnp.zeros_like(work)
    pl.semaphore_wait(barrier, 5)

    low, high = pl.ds(0, HALO), pl.ds(HALO, HALO)
    kap_copies = (
        remote(kappa.at[high], kap.at[pl.ds(0, HALO)], kap_sem.at[0], kap_sem.at[1], north),
        remote(kappa.at[low], kap.at[pl.ds(HALO + ROWS, HALO)], kap_sem.at[2], kap_sem.at[3], south),
    )

    def edges(src, dst, send, recv, off):
        z = at(off)
        j = off % RING
        return (
            remote(src.at[:, :, z, high], dst.at[:, :, z, high], send.at[j, 0], recv.at[j, 0], north),
            remote(src.at[:, :, z, low], dst.at[:, :, z, low], send.at[j, 1], recv.at[j, 1], south),
        )

    forward = {off: edges(alpha, halo_f, hf_send, hf_recv, off) for off in NEAR_LAST}
    backward = {off: edges(back, halo_b, hb_send, hb_recv, off) for off in NEAR_LAST}
    observed = (
        remote(weight, obs.at[pair, 0], ob_send.at[0], ob_recv.at[0], opposite),
        remote(innov, obs.at[pair, 1], ob_send.at[1], ob_recv.at[1], opposite),
    )
    scatter = {
        (way, k, t): remote(
            ring.at[way, k, t], ring.at[way, k - 1, t],
            rs_send.at[way, k - 1, t], rs_recv.at[way, k - 1, t], toward[way],
        )
        for way in (DOWN, UP) for t in range(SLOTS) for k in range(1, REACH[way][t] + 1)
    }
    cross = [remote(total.at[t], across.at[t], x_send.at[t], x_recv.at[t], opposite) for t in range(SLOTS)]

    def gather_copy(way, k, t):
        z = at(k if way == DOWN else -k)
        return remote(
            misfit.at[z, t], misfit.at[z, t], ag_send.at[way, k, t], ag_recv.at[way, k, t], toward[way]
        )

    gather = {
        (way, k, t): gather_copy(way, k, t)
        for way in (DOWN, UP) for t in range(SLOTS) for k in range(REACH[way][t])
    }

    def send_edges(copies):
        for copy in copies:
            go(copy)

    send_edges(kap_copies)
    send_edges(forward[NEAR_LAST[0]])

    loads[0].wait()
    for copy in kap_copies:
        copy.wait_recv()
    send_edges(forward[NEAR_LAST[1]])
    row = lax.broadcasted_iota(jnp.int32, (2 * ROWS, LON), 0)
    row8 = lax.broadcasted_iota(jnp.int32, (LON // LANES, ROWS, LANES), 1)
    known = ((row8 < HALO) & (space < SPACE - 1)) | ((row8 >= HALO) & (space > 0))

    def apart(x):
        return jnp.stack([x[:, n * LANES : (n + 1) * LANES] for n in range(LON // LANES)])

    inside = ((row >= HALO) | (space > 0)) & ((row < HALO + ROWS) | (space < SPACE - 1))
    k16 = jnp.where(inside, kap[...], 0.0)
    east = 0.5 * (k16 + pltpu.roll(k16, LON - 1, 1))
    west = 0.5 * (k16 + pltpu.roll(k16, 1, 1))
    up = 0.5 * (k16 + pltpu.roll(k16, 2 * ROWS - 1, 0))
    down = 0.5 * (k16 + pltpu.roll(k16, 1, 0))
    for i, c in enumerate((1.0 - (east + west + up + down), east, west, up, down)):
        c = jnp.where(inside, c, 0.0)
        coef[i] = apart(c)
        coef_own[i] = apart(c[HALO : HALO + ROWS])
    send_edges(forward[NEAR_LAST[2]])
    loads[2].wait()
    sea[...] = sea_i[...].astype(jnp.float32)

    count = LON // LANES
    lane = lax.broadcasted_iota(jnp.int32, (count, ROWS, LANES), 2)

    def smooth(tiles, edges, store):
        for f, (tile, edge) in enumerate(zip(tiles, edges)):
            work[0, f, :, FIRST + HALO : FIRST + HALO + ROWS] = apart(tile)
            edge = jnp.where(known, apart(edge), 0.0)
            work[0, f, :, FIRST : FIRST + HALO] = edge[:, HALO:]
            work[0, f, :, FIRST + HALO + ROWS : FIRST + 2 * ROWS] = edge[:, :HALO]
        for step in range(STEPS):
            now, later = step % 2, 1 - step % 2
            last = step == STEPS - 1
            starts = (FIRST + HALO,) if last else (FIRST, FIRST + ROWS)
            table = coef_own if last else coef
            for f in range(len(tiles)):
                for i, start in enumerate(starts):
                    u = work[now, f, :, pl.ds(start, ROWS)]
                    ahead = jnp.concatenate([u[1:], u[:1]], axis=0)
                    behind = jnp.concatenate([u[-1:], u[:-1]], axis=0)
                    terms = (
                        u,
                        pltpu.roll(jnp.where(lane == 0, ahead, u), LANES - 1, 2),
                        pltpu.roll(jnp.where(lane == LANES - 1, behind, u), 1, 2),
                        work[now, f, :, pl.ds(start + 1, ROWS)],
                        work[now, f, :, pl.ds(start - 1, ROWS)],
                    )
                    t = [table[q, :, pl.ds(i * ROWS, ROWS)] * term for q, term in enumerate(terms)]
                    value = ((t[0] + t[1]) + (t[2] + t[3])) + t[4]
                    if last:
                        store(f, jnp.concatenate([value[n] for n in range(count)], axis=1))
                    else:
                        work[later, f, :, pl.ds(start, ROWS)] = value

    def diffuse_forward(off):
        for copy in forward[off]:
            copy.wait_recv()
        z = at(off)

        def store(f, value):
            m, p = FIELDS[f]
            local[m, p, z] = value * sea[...]

        smooth([al[m, p, z] for m, p in FIELDS], [halo_f[m, p, z] for m, p in FIELDS], store)

    def partial(off, t, p):
        z = at(off)
        return (
            pe[t, 0, p, z].astype(jnp.float32) * local[0, p, z]
            + pe[t, 1, p, z].astype(jnp.float32) * local[1, p, z]
        )

    def scatter_step(way, k, t):
        off = -k if way == DOWN else k
        if k < REACH[way][t]:
            scatter[way, k + 1, t].wait_recv()
        for p in range(PAIR):
            part = partial(off, t, p)
            if k < REACH[way][t]:
                part = part + ring[way, k, t, p]
            ring[way, k, t, p] = part
        go(scatter[way, k, t])

    def cross_step(t):
        for way in (DOWN, UP):
            scatter[way, 1, t].wait_recv()
        for p in range(PAIR):
            total[t, p] = partial(0, t, p) + ring[DOWN, 0, t, p] + ring[UP, 0, t, p]
        go(cross[t])

    stored = []

    def misfit_step(t):
        cross[t].wait_recv()
        for p in range(PAIR):
            misfit[depth, t, p] = obs[p, 0, t] * (total[t, p] + across[t, p] - obs[p, 1, t])
        for way in (DOWN, UP):
            go(gather[way, 0, t])
        copy = pltpu.make_async_copy(misfit.at[depth, t, pair], misfit_out.at[t], out_sem.at[RING + t])
        copy.start()
        stored.append(copy)

    def relay(way, k, t):
        gather[way, k - 1, t].wait_recv()
        if k < REACH[way][t]:
            go(gather[way, k, t])

    def adjoint(off):
        z = at(off)

        @pl.loop(0, OWN * PAIR)
        def _(i):
            m, p = i // PAIR, lax.rem(i, PAIR)
            acc = pe[0, m, p, z].astype(jnp.float32) * misfit[z, 0, p]
            for t in range(1, SLOTS):
                acc = acc + pe[t, m, p, z].astype(jnp.float32) * misfit[z, t, p]
            back[m, p, z] = acc * sea[...]

        send_edges(backward[off])

    def diffuse_backward(off):
        for copy in backward[off]:
            copy.wait_recv()
        z = at(off)

        def store(f, value):
            m, p = FIELDS[f]
            result[m, p, z] = value + al[m, p, z]

        smooth([back[m, p, z] for m, p in FIELDS], [halo_b[m, p, z] for m, p in FIELDS], store)

        copy = pltpu.make_async_copy(result.at[:, :, z], grad_out.at[:, :, z], out_sem.at[off % RING])
        copy.start()
        stored.append(copy)

    tasks = {
        "load": lambda i: loads[i].wait(),
        "edges": lambda off: send_edges(forward[off]),
        "forward": diffuse_forward,
        "scatter": scatter_step,
        "observe": lambda: send_edges(observed),
        "observed": lambda: [copy.wait_recv() for copy in observed],
        "cross": cross_step,
        "misfit": misfit_step,
        "relay": relay,
        "adjoint": adjoint,
        "backward": diffuse_backward,
    }
    for name, *details in ORDER:
        tasks[name](*details)

    for copy in sent:
        copy.wait_send()
    for copy in stored:
        copy.wait()


def finish(grad, misfit, grad_out, misfit_out, held, held_misfit, in_sem, out_sem):
    routes = [(misfit, held_misfit, misfit_out)]
    routes += [(grad.at[m, p], held.at[m, p], grad_out.at[m, p]) for m, p in FIELDS]
    arrive = [pltpu.make_async_copy(a, b, in_sem.at[i]) for i, (a, b, c) in enumerate(routes)]
    leave = [pltpu.make_async_copy(b, c, out_sem.at[i]) for i, (a, b, c) in enumerate(routes)]
    for copy in arrive:
        copy.start()
    for first, second in zip(arrive, leave):
        first.wait()
        second.start()
    for copy in leave:
        copy.wait()


def body(alpha, perturb, kappa, land, obs_weight, innovation):
    f32, dma = jnp.float32, pltpu.SemaphoreType.DMA
    field = (OWN, PAIR, RING, ROWS, LON)
    slab = (SLOTS, PAIR, ROWS, LON)
    anywhere = pl.BlockSpec(memory_space=pltpu.HBM)
    grad, misfit = pl.pallas_call(
        kernel,
        out_shape=(
            jax.ShapeDtypeStruct(field, f32),
            jax.ShapeDtypeStruct((SLOTS, ROWS, LON), f32),
        ),
        in_specs=[anywhere] * 6,
        out_specs=(anywhere, anywhere),
        scratch_shapes=[
            pltpu.VMEM(field, f32),
            pltpu.VMEM((SLOTS,) + field, jnp.bfloat16),
            pltpu.VMEM(field, f32),
            pltpu.VMEM(field, f32),
            pltpu.VMEM(field, f32),
            pltpu.VMEM(field, f32),
            pltpu.VMEM((2, OWN * PAIR, LON // LANES, 3 * ROWS, LANES), f32),
            pltpu.VMEM((2 * ROWS, LON), f32),
            pltpu.VMEM((5, LON // LANES, 2 * ROWS, LANES), f32),
            pltpu.VMEM((5, LON // LANES, ROWS, LANES), f32),
            pltpu.VMEM((ROWS, LON), jnp.int32),
            pltpu.VMEM((ROWS, LON), f32),
            pltpu.VMEM(field, f32),
            pltpu.VMEM((2, 5) + slab, f32),
            pltpu.VMEM(slab, f32),
            pltpu.VMEM(slab, f32),
            pltpu.VMEM((PAIR, 2, SLOTS, ROWS, LON), f32),
            pltpu.VMEM((RING,) + slab, f32),
            dma((6,)),
            dma((RING + SLOTS,)),
            dma((4,)),
            dma((RING, 2)),
            dma((RING, 2)),
            dma((RING, 2)),
            dma((RING, 2)),
            dma((2, 4, SLOTS)),
            dma((2, 4, SLOTS)),
            dma((SLOTS,)),
            dma((SLOTS,)),
            dma((2,)),
            dma((2,)),
            dma((2, 4, SLOTS)),
            dma((2, 4, SLOTS)),
        ],
        compiler_params=pltpu.CompilerParams(
            collective_id=0, has_side_effects=True, vmem_limit_bytes=60 * 2**20
        ),
    )(
        alpha.reshape(field),
        perturb.reshape((SLOTS,) + field),
        kappa,
        land,
        obs_weight.reshape(SLOTS, ROWS, LON),
        innovation.reshape(SLOTS, ROWS, LON),
    )
    grad, misfit = pl.pallas_call(
        finish,
        out_shape=(
            jax.ShapeDtypeStruct(field, f32),
            jax.ShapeDtypeStruct((SLOTS, ROWS, LON), f32),
        ),
        in_specs=[anywhere] * 2,
        out_specs=(anywhere, anywhere),
        scratch_shapes=[
            pltpu.VMEM(field, f32),
            pltpu.VMEM((SLOTS, ROWS, LON), f32),
            dma((len(FIELDS) + 1,)),
            dma((len(FIELDS) + 1,)),
        ],
        compiler_params=pltpu.CompilerParams(vmem_limit_bytes=60 * 2**20),
    )(grad, misfit)
    return grad.reshape(alpha.shape), misfit.reshape(obs_weight.shape)


def solution(mesh):
    placed = (
        P("member", None, "space", None),
        P(None, "member", None, "space", None),
        P("space", None),
        P("space", None),
        P(None, "member", "space", None),
        P(None, "member", "space", None),
    )
    return jax.shard_map(
        body,
        mesh=mesh,
        in_specs=placed,
        out_specs=(P("member", None, "space", None), P(None, "member", "space", None)),
        check_vma=False,
    )
```
